128 devices in a mesh: dp: 32 (over x, y, core), mp: 4 (over z).
Axes of the slice: x: 4, y: 4, z: 4, core: 2. Of those that a mesh axis runs over, the one named last changes fastest.
Arguments:
- embeddings: bfloat16 [262144, 2560], P('dp', 'mp')
- centroids: bfloat16 [65536, 2560], P(('dp', 'mp'))
- labels: bfloat16 [65536, 1024], P(('dp', 'mp')), may hold values from -12 to 12
- candidates: int32 [1024, 8], P(('dp', 'mp')), may hold values from 0 to 511, as said below
- counts: int32 [1024], P(('dp', 'mp')), may hold values from 4 to 8, as said below
- home: int32 [512], replicated, may hold values from 0 to 511, as said below
Outputs:
- profiles: bfloat16 [262144, 1024], P(('dp', 'mp'))
The draws below stay inside these ranges and needn't reach their ends.
Inputs may be any that keep to these rules, and one draw needn't show every extreme that they name: `home`: a permutation of the tiles. `candidates`: candidate tile ids are distinct within a block; entries from position counts[b] on are padding; the candidate tiles of the 8 blocks of one device, padding included, are exactly one tile stored on each device with the same mp index. `counts`: some block of every device has 8.
All inputs are finite; a program needn't handle non-finite values.
Results may differ from the reference program's by a relative error of at most 0.0048.
Values may be sent and summed in bfloat16 or wider, within the bound.
No kernel may reach another device: no remote copies, remote signals or barrier semaphores. Data moves between devices by JAX's collectives and lax.ppermute only.
A program may use at most 192 MiB of HBM per device.

```python
import math
import jax
import jax.numpy as jnp
from jax import lax

D = 2560
LAB = 1024
TR = 128
BR = 256
CAND = 8
CMIN = 4
TILE_DEV = 4
BLK_DEV = 8
TILES = 512
BLOCKS = 1024
TOKENS = 262144
N_DP = 32
N_MP = 4
DEVICES = 128


def routing(key):
    base = jax.random.fold_in(key, 101)
    home = jax.random.permutation(jax.random.fold_in(base, 1), TILES).astype(jnp.int32)
    inverse = jnp.zeros((TILES,), jnp.int32).at[home].set(jnp.arange(TILES, dtype=jnp.int32))
    picks = jax.random.randint(jax.random.fold_in(base, 2), (DEVICES, N_DP), 0, TILE_DEV).astype(jnp.int32)
    pool_keys = jax.random.split(jax.random.fold_in(base, 3), DEVICES)
    pools = jax.vmap(lambda k: jax.random.permutation(k, N_DP))(pool_keys).astype(jnp.int32)
    rest_keys = jax.random.split(jax.random.fold_in(base, 4), BLOCKS)
    rests = jax.vmap(lambda k: jax.random.permutation(k, N_DP - CMIN)[:CAND - CMIN])(rest_keys).astype(jnp.int32)
    block_ids = jnp.arange(BLOCKS, dtype=jnp.int32)
    device = block_ids // BLK_DEV
    within = block_ids % BLK_DEV
    first = within[:, None] * CMIN + jnp.arange(CMIN, dtype=jnp.int32)[None, :]
    later = within[:, None] * CMIN + CMIN + rests
    position = jnp.concatenate([first, later], axis=1) % N_DP
    owner = jnp.take_along_axis(pools[device], position, axis=1)
    column = device % N_MP
    local = jnp.take_along_axis(picks[device], owner, axis=1)
    storage = (owner * N_MP + column[:, None]) * TILE_DEV + local
    candidates = inverse[storage]
    live_counts = jax.random.randint(jax.random.fold_in(base, 5), (BLOCKS,), CMIN, CAND + 1).astype(jnp.int32)
    fullest = jax.random.randint(jax.random.fold_in(base, 6), (DEVICES,), 0, BLK_DEV).astype(jnp.int32)
    live_counts = jnp.where(within == fullest[device], CAND, live_counts).astype(jnp.int32)
    return (home, candidates.astype(jnp.int32), live_counts)


def centroid_parts(key):
    base = jax.random.fold_in(key, 202)
    raw = jax.random.normal(jax.random.fold_in(base, 1), (TILES * TR, D), jnp.float32)
    logscale = jax.random.uniform(jax.random.fold_in(base, 2), (TILES * TR, 1), jnp.float32, math.log(0.5), math.log(1.5))
    scales = jnp.exp(logscale)
    return raw * scales


def draw_home(key, part):
    return routing(key)[0]


def draw_candidates(key, part):
    return routing(key)[1]


def draw_counts(key, part):
    return routing(key)[2]


def draw_centroids(key, part):
    return centroid_parts(key).astype(jnp.bfloat16)


def draw_embeddings(key, part):
    base = jax.random.fold_in(key, 303)
    values = jax.random.normal(jax.random.fold_in(base, 1), (TOKENS, D), jnp.float32)
    return values.astype(jnp.bfloat16)


def levels(own_key, extent, shards, low, top_value):
    gain, own = 1.0, jax.random.fold_in(own_key, 6)
    for dim, blocks in shards:
        steps = jnp.exp(jax.random.uniform(jax.random.fold_in(own, dim), (blocks,), jnp.float32, low / len(shards), top_value / len(shards)))
        gain = gain * jnp.repeat(steps, extent[dim] // blocks).reshape([-1 if axis == dim else 1 for axis in range(len(extent))])
    return gain


def noise(own_key, extent, scale, most, pieces=(), kind=jnp.bfloat16):
    factor_of = levels(own_key, extent, pieces, -0.22, 0.18) if pieces else 1.0
    drawn = jax.random.normal(own_key, extent, jnp.float32) * scale * factor_of
    return jnp.minimum(jnp.maximum(drawn, -most), most).astype(kind)


def setup_inputs(seed: int = 0) -> dict:
    splits = jax.random.split(jax.random.key(seed), 7)
    return {
        "embeddings": draw_embeddings(jax.random.fold_in(splits[6], 71), 0),
        "centroids": draw_centroids(jax.random.fold_in(splits[6], 71), 0),
        "labels": noise(splits[2], (TILES * TR, LAB), 2.0, 12.0, ((0, 128),)),
        "candidates": draw_candidates(jax.random.fold_in(splits[6], 71), 0),
        "counts": draw_counts(jax.random.fold_in(splits[6], 71), 0),
        "home": draw_home(jax.random.fold_in(splits[6], 71), 0),
    }


def reference(embeddings, centroids, labels, candidates, counts, home):
    tile_total = home.shape[0]
    cent_tiles = centroids.reshape(tile_total, TR, D)
    label_tiles = labels.reshape(tile_total, TR, LAB)
    storage = home[candidates].astype(jnp.int32)
    block_rows = embeddings.reshape(BLOCKS, BR, D)
    scale = 2.0 / math.sqrt(D)

    def one_block(items):
        rows, slots, count = items
        chosen = cent_tiles[slots].astype(jnp.float32)
        chosen_labels = label_tiles[slots].astype(jnp.float32)
        logits = jnp.einsum('rd,ctd->rct', rows.astype(jnp.float32), chosen) * scale
        live = (jnp.arange(CAND, dtype=jnp.int32) < count)[None, :, None]
        logits = jnp.where(live, logits, -jnp.inf)
        peak = lax.optimization_barrier(jnp.max(logits, axis=(1, 2), keepdims=True))
        weights = jnp.exp(logits - peak)
        total = lax.optimization_barrier(jnp.sum(weights, axis=(1, 2), keepdims=True))
        probs = (weights / total).astype(jnp.bfloat16)
        result = jnp.einsum('rct,ctl->rl', probs.astype(jnp.float32), chosen_labels)
        return result.astype(jnp.bfloat16)
    result = lax.map(one_block, (block_rows, storage, counts))
    return result.reshape(BLOCKS * BR, LAB)
```

```python
import functools
import math

import jax
import jax.numpy as jnp
from jax import lax
from jax.experimental import pallas as pl
from jax.experimental.pallas import tpu as pltpu
from jax.sharding import PartitionSpec as P

D = 2560
LAB = 1024
TR = 128
HR = TR // 2
BR = 256
CAND = 8
NX = 4
NY = 4
NC = 2
NZ = 4
NDP = NX * NY * NC
TILE_DEV = 4
BLK_DEV = 8
WIDE = D + LAB
PIECE = D // NZ
ROWS = BLK_DEV * BR
HBM = pl.BlockSpec(memory_space=pl.ANY)
SMEM = pl.BlockSpec(memory_space=pltpu.SMEM)


def dp_index(x, y, c):
    return ((x % NX) * NY + (y % NY)) * NC + c


def shift(value, dx, dy, flip):
    pairs = [
        (dp_index(x, y, c), dp_index(x + dx, y + dy, c ^ flip))
        for x in range(NX)
        for y in range(NY)
        for c in range(NC)
    ]
    return lax.ppermute(value, "dp", pairs)


def pick_kernel(targets, table, place, *refs):
    held = (refs[0:5], refs[5:10])
    outs = refs[10:-1]
    sem = refs[-1]
    x, y, c = place[0], place[1], place[2]
    count = 0
    for side in range(2):
        own, before, after, low, high = held[side]
        for step, flip in targets:
            out = outs[count // 4]
            for r in range(4):
                if side == 0:
                    target = (x * NY + ((y + step) & 3)) * NC + (c ^ flip)
                    owner = (((x + r) & 3) * NY + y) * NC + c
                else:
                    target = (((x + step) & 3) * NY + y) * NC + (c ^ flip)
                    owner = (x * NY + ((y + r) & 3)) * NC + c
                w = table[target, owner]
                if r == 2:

                    @pl.when(w < 2)
                    def _():
                        pltpu.make_async_copy(low.at[jnp.minimum(w, 1)], out.at[r], sem.at[count]).start()

                    @pl.when(w >= 2)
                    def _():
                        pltpu.make_async_copy(high.at[jnp.maximum(w - 2, 0)], out.at[r], sem.at[count]).start()
                else:
                    source = (own, after, None, before)[r]
                    pltpu.make_async_copy(source.at[w], out.at[r], sem.at[count]).start()
                count += 1
    for i in range(count):
        pltpu.make_async_copy(held[0][0].at[0], outs[i // 4].at[i % 4], sem.at[i]).wait()


def pick(targets, table, place, held):
    sends = 2 * len(targets)
    shape = jax.ShapeDtypeStruct((4, HR, WIDE), jnp.bfloat16)
    size = sends * 4 * HR * WIDE * 2
    return pl.pallas_call(
        functools.partial(pick_kernel, targets),
        out_shape=[shape] * sends,
        in_specs=[SMEM, SMEM] + [HBM] * 10,
        out_specs=[HBM] * sends,
        scratch_shapes=[pltpu.SemaphoreType.DMA((sends * 4,))],
        cost_estimate=pl.CostEstimate(flops=0, bytes_accessed=2 * size, transcendentals=0),
    )(table, place, *held)


def score_kernel(owners, fresh, counts, place, *refs):
    got = (refs[0:8], refs[8:16])
    parts = refs[16:20]
    out = refs[20]
    cents, labs, rows, logits, tile_sem, row_sem = refs[21:]
    b = pl.program_id(0)
    x, y, c, z = place[0], place[1], place[2], place[3]

    def tile_copies(side, k, r, o):
        source = got[side][k]
        half = pl.ds(side * HR, HR)
        return (
            pltpu.make_async_copy(
                source.at[r, :, pl.ds(0, D)], cents.at[o, half, :], tile_sem.at[2 * side, o]
            ),
            pltpu.make_async_copy(
                source.at[r, :, pl.ds(D, LAB)], labs.at[o, half, :], tile_sem.at[2 * side + 1, o]
            ),
        )

    def fetch(block):
        def one(j, carry):
            at = block * CAND + j

            @pl.when(fresh[at] > 0)
            def _():
                o = owners[at]
                rx = ((o >> 3) - x) & 3
                ry = ((o >> 1) - y) & 3
                rc = (o & 1) ^ c
                for side, near, r in ((0, ry, rx), (1, rx, ry)):
                    which = near * 2 + rc
                    for k in range(8):

                        @pl.when(which == k)
                        def _():
                            for copy in tile_copies(side, k, r, o):
                                copy.start()

            return carry

        lax.fori_loop(0, CAND, one, 0)

    def row_copies(block):
        slot = lax.rem(block, 2)
        for r in range(NZ):
            start = block * BR + (z * ROWS if r == 0 else 0)
            column = pl.multiple_of(((z + r) & 3) * PIECE, 128)
            yield pltpu.make_async_copy(
                parts[r].at[pl.ds(pl.multiple_of(start, BR), BR), :],
                rows.at[slot, :, pl.ds(column, PIECE)],
                row_sem.at[slot, r],
            )

    @pl.when(b == 0)
    def _():
        for copy in row_copies(b):
            copy.start()
        fetch(b)

    @pl.when(b + 1 < BLK_DEV)
    def _():
        for copy in row_copies(b + 1):
            copy.start()
        fetch(b + 1)

    for copy in row_copies(b):
        copy.wait()

    def settle(j, carry):
        at = b * CAND + j

        @pl.when(fresh[at] > 0)
        def _():
            o = owners[at]
            for side in range(2):
                for copy in tile_copies(side, 0, 0, o):
                    copy.wait()

        return carry

    lax.fori_loop(0, CAND, settle, 0)

    live = counts[b]
    members = rows.at[lax.rem(b, 2)]
    scale = 2.0 / math.sqrt(D)
    for pair in range(CAND // 2):
        columns = slice(pair * 2 * TR, (pair + 1) * 2 * TR)

        @pl.when(2 * pair < live)
        def _():
            first = owners[b * CAND + 2 * pair]
            second = owners[b * CAND + 2 * pair + 1]
            tiles = jnp.concatenate([cents[first], cents[second]], axis=0)
            value = lax.dot_general(
                members[...], tiles, (((1,), (1,)), ((), ())), preferred_element_type=jnp.float32
            )
            column = lax.broadcasted_iota(jnp.int32, (BR, 2 * TR), 1) + pair * 2 * TR
            logits[:, columns] = jnp.where(column < live * TR, value * scale, -jnp.inf)

        @pl.when(2 * pair >= live)
        def _():
            logits[:, columns] = jnp.full((BR, 2 * TR), -jnp.inf, jnp.float32)

    value = logits[...]
    peak = jnp.max(value, axis=1, keepdims=True)
    weights = jnp.exp(value - peak)
    total = jnp.sum(weights, axis=1, keepdims=True)
    probs = (weights / total).astype(jnp.bfloat16)
    tiles = jnp.concatenate([labs[owners[b * CAND + j]] for j in range(CAND)], axis=0)
    result = jnp.dot(probs, tiles, preferred_element_type=jnp.float32)
    out[...] = result.astype(jnp.bfloat16)


def score(owners, fresh, counts, place, got, parts):
    return pl.pallas_call(
        score_kernel,
        out_shape=jax.ShapeDtypeStruct((ROWS, LAB), jnp.bfloat16),
        grid_spec=pltpu.PrefetchScalarGridSpec(
            num_scalar_prefetch=4,
            grid=(BLK_DEV,),
            in_specs=[HBM] * 20,
            out_specs=pl.BlockSpec((BR, LAB), lambda b, *_: (b, 0)),
            scratch_shapes=[
                pltpu.VMEM((NDP, TR, D), jnp.bfloat16),
                pltpu.VMEM((NDP, TR, LAB), jnp.bfloat16),
                pltpu.VMEM((2, BR, D), jnp.bfloat16),
                pltpu.VMEM((BR, CAND * TR), jnp.float32),
                pltpu.SemaphoreType.DMA((4, NDP)),
                pltpu.SemaphoreType.DMA((2, NZ)),
            ],
        ),
        compiler_params=pltpu.CompilerParams(
            dimension_semantics=("arbitrary",), vmem_limit_bytes=56 * 1024 * 1024
        ),
        cost_estimate=pl.CostEstimate(
            flops=2 * ROWS * CAND * TR * WIDE,
            bytes_accessed=NDP * TR * WIDE * 2 + ROWS * WIDE * 2,
            transcendentals=ROWS * CAND * TR,
        ),
    )(owners, fresh, counts, place, *got, *parts)


def body(embeddings, centroids, labels, candidates, counts, home):
    me = lax.axis_index("dp")
    z = lax.axis_index("mp")
    place = jnp.stack([me // (NY * NC), (me // NC) % NY, me % NC, z]).astype(jnp.int32)

    tiles = centroids.reshape(TILE_DEV, TR, D)
    tile_labels = labels.reshape(TILE_DEV, TR, LAB)
    own = [
        jnp.concatenate([tiles[:, s : s + HR], tile_labels[:, s : s + HR]], axis=2) for s in (0, HR)
    ]
    held = []
    for side in range(2):
        dx, dy = ((1, 0), (0, 1))[side]
        before = shift(own[side], dx, dy, 0)
        after = shift(own[side], -dx, -dy, 0)
        low = shift(before[:2], dx, dy, 0)
        high = shift(after[2:], -dx, -dy, 0)
        held += [own[side], before, after, low, high]

    identity = jnp.arange(home.shape[0], dtype=jnp.int32)
    storage = jnp.sum(jnp.where(candidates[:, :, None] == identity, home, 0), axis=2)
    owner = storage // (TILE_DEV * NZ)
    local = storage % TILE_DEV
    hit = owner.reshape(-1)[:, None] == jnp.arange(NDP, dtype=jnp.int32)[None, :]
    wanted = jnp.max(jnp.where(hit, local.reshape(-1)[:, None], 0), axis=0)
    table = lax.all_gather(wanted, "dp")

    parts = [embeddings]
    for r in range(1, NZ):
        target = (z - r) % NZ
        piece = lax.dynamic_slice_in_dim(embeddings, target * ROWS, ROWS, 0)
        parts.append(lax.ppermute(piece, "mp", [(i, (i - r) % NZ) for i in range(NZ)]))

    got = [[None] * 8, [None] * 8]
    for targets in (((1, 0), (3, 0)), ((1, 1), (3, 1)), ((2, 0), (2, 1)), ((0, 0), (0, 1))):
        sends = pick(targets, table, place, held)
        for side in range(2):
            for i, (step, flip) in enumerate(targets):
                value = sends[side * len(targets) + i]
                if (step, flip) != (0, 0):
                    value = shift(value, step * side, step * (1 - side), flip)
                got[side][((-step) % 4) * 2 + flip] = value

    live = jnp.arange(CAND, dtype=jnp.int32)[None, :] < counts[:, None]
    slots = jnp.where(live, owner, owner[:, :1])
    flat = slots.reshape(-1)
    order = jnp.arange(BLK_DEV * CAND, dtype=jnp.int32) // CAND
    seen = (flat[:, None] == flat[None, :]) & (order[None, :] < order[:, None])
    fresh = (live.reshape(-1) & ~jnp.any(seen, axis=1)).astype(jnp.int32)
    return score(flat, fresh, counts, place, got[0] + got[1], parts)


def solution(mesh):
    placed = (
        P("dp", "mp"),
        P(("dp", "mp"), None),
        P(("dp", "mp"), None),
        P(("dp", "mp"), None),
        P(("dp", "mp")),
        P(),
    )
    return jax.shard_map(
        body, mesh=mesh, in_specs=placed, out_specs=P(("dp", "mp"), None), check_vma=False
    )
```

```python
import functools
import math

import jax
import jax.numpy as jnp
from jax import lax
from jax.experimental import pallas as pl
from jax.experimental.pallas import tpu as pltpu
from jax.sharding import PartitionSpec as P

D = 2560
LAB = 1024
TR = 128
HR = TR // 2
BR = 256
CAND = 8
NX = 4
NY = 4
NC = 2
NZ = 4
NDP = NX * NY * NC
TILE_DEV = 4
BLK_DEV = 8
WIDE = D + LAB
PIECE = D // NZ
ROWS = BLK_DEV * BR
HBM = pl.BlockSpec(memory_space=pl.ANY)
SMEM = pl.BlockSpec(memory_space=pltpu.SMEM)


def dp_index(x, y, c):
    return ((x % NX) * NY + (y % NY)) * NC + c


def shift(value, dx, dy, flip):
    pairs = [
        (dp_index(x, y, c), dp_index(x + dx, y + dy, c ^ flip))
        for x in range(NX)
        for y in range(NY)
        for c in range(NC)
    ]
    return lax.ppermute(value, "dp", pairs)


def pick_kernel(targets, table, place, *refs):
    held = (refs[0:5], refs[5:10])
    outs = refs[10:-3]
    stage, sem, out_sem = refs[-3:]
    x, y, c = place[0], place[1], place[2]
    count = 0
    for side in range(2):
        own, before, after, low, high = held[side]
        for step, flip in targets:
            for r in range(4):
                if side == 0:
                    target = (x * NY + ((y + step) & 3)) * NC + (c ^ flip)
                    owner = (((x + r) & 3) * NY + y) * NC + c
                else:
                    target = (((x + step) & 3) * NY + y) * NC + (c ^ flip)
                    owner = (x * NY + ((y + r) & 3)) * NC + c
                w = table[target, owner]
                if r == 2:

                    @pl.when(w < 2)
                    def _():
                        pltpu.make_async_copy(low.at[jnp.minimum(w, 1)], stage.at[count], sem.at[count]).start()

                    @pl.when(w >= 2)
                    def _():
                        pltpu.make_async_copy(high.at[jnp.maximum(w - 2, 0)], stage.at[count], sem.at[count]).start()
                else:
                    source = (own, after, None, before)[r]
                    pltpu.make_async_copy(source.at[w], stage.at[count], sem.at[count]).start()
                count += 1
    for i in range(count):
        pltpu.make_async_copy(held[0][0].at[0], stage.at[i], sem.at[i]).wait()
        pltpu.make_async_copy(stage.at[i], outs[i // 4].at[i % 4], out_sem.at[i]).start()
    for i in range(count):
        pltpu.make_async_copy(stage.at[i], outs[i // 4].at[i % 4], out_sem.at[i]).wait()


def pick(targets, table, place, held):
    sends = 2 * len(targets)
    shape = jax.ShapeDtypeStruct((4, HR, WIDE), jnp.bfloat16)
    size = sends * 4 * HR * WIDE * 2
    return pl.pallas_call(
        functools.partial(pick_kernel, targets),
        out_shape=[shape] * sends,
        in_specs=[SMEM, SMEM] + [HBM] * 10,
        out_specs=[HBM] * sends,
        scratch_shapes=[
            pltpu.VMEM((sends * 4, HR, WIDE), jnp.bfloat16),
            pltpu.SemaphoreType.DMA((sends * 4,)),
            pltpu.SemaphoreType.DMA((sends * 4,)),
        ],
        compiler_params=pltpu.CompilerParams(vmem_limit_bytes=12 * 1024 * 1024),
        cost_estimate=pl.CostEstimate(flops=0, bytes_accessed=2 * size, transcendentals=0),
    )(table, place, *held)


def score_kernel(owners, fresh, counts, place, *refs):
    got = (refs[0:8], refs[8:16])
    parts = refs[16:20]
    out = refs[20]
    cents, labs, rows, logits, tile_sem, row_sem = refs[21:]
    b = pl.program_id(0)
    x, y, c, z = place[0], place[1], place[2], place[3]

    def tile_copies(side, k, r, o):
        source = got[side][k]
        half = pl.ds(side * HR, HR)
        return (
            pltpu.make_async_copy(
                source.at[r, :, pl.ds(0, D)], cents.at[o, half, :], tile_sem.at[2 * side, o]
            ),
            pltpu.make_async_copy(
                source.at[r, :, pl.ds(D, LAB)], labs.at[o, half, :], tile_sem.at[2 * side + 1, o]
            ),
        )

    def fetch(block):
        def one(j, carry):
            at = block * CAND + j

            @pl.when(fresh[at] > 0)
            def _():
                o = owners[at]
                rx = ((o >> 3) - x) & 3
                ry = ((o >> 1) - y) & 3
                rc = (o & 1) ^ c
                for side, near, r in ((0, ry, rx), (1, rx, ry)):
                    which = near * 2 + rc
                    for k in range(8):

                        @pl.when(which == k)
                        def _():
                            for copy in tile_copies(side, k, r, o):
                                copy.start()

            return carry

        lax.fori_loop(0, CAND, one, 0)

    def row_copies(block):
        slot = lax.rem(block, 2)
        for r in range(NZ):
            start = block * BR + (z * ROWS if r == 0 else 0)
            column = pl.multiple_of(((z + r) & 3) * PIECE, 128)
            yield pltpu.make_async_copy(
                parts[r].at[pl.ds(pl.multiple_of(start, BR), BR), :],
                rows.at[slot, :, pl.ds(column, PIECE)],
                row_sem.at[slot, r],
            )

    @pl.when(b == 0)
    def _():
        for copy in row_copies(b):
            copy.start()
        fetch(b)

    @pl.when(b + 1 < BLK_DEV)
    def _():
        for copy in row_copies(b + 1):
            copy.start()
        fetch(b + 1)

    for copy in row_copies(b):
        copy.wait()

    def settle(j, carry):
        at = b * CAND + j

        @pl.when(fresh[at] > 0)
        def _():
            o = owners[at]
            for side in range(2):
                for copy in tile_copies(side, 0, 0, o):
                    copy.wait()

        return carry

    lax.fori_loop(0, CAND, settle, 0)

    live = counts[b]
    members = rows.at[lax.rem(b, 2)]
    scale = 2.0 / math.sqrt(D)
    for pair in range(CAND // 2):
        columns = slice(pair * 2 * TR, (pair + 1) * 2 * TR)

        @pl.when(2 * pair < live)
        def _():
            first = owners[b * CAND + 2 * pair]
            second = owners[b * CAND + 2 * pair + 1]
            tiles = jnp.concatenate([cents[first], cents[second]], axis=0)
            value = lax.dot_general(
                members[...], tiles, (((1,), (1,)), ((), ())), preferred_element_type=jnp.float32
            )
            column = lax.broadcasted_iota(jnp.int32, (BR, 2 * TR), 1) + pair * 2 * TR
            logits[:, columns] = jnp.where(column < live * TR, value * scale, -jnp.inf)

        @pl.when(2 * pair >= live)
        def _():
            logits[:, columns] = jnp.full((BR, 2 * TR), -jnp.inf, jnp.float32)

    value = logits[...]
    peak = jnp.max(value, axis=1, keepdims=True)
    weights = jnp.exp(value - peak)
    total = jnp.sum(weights, axis=1, keepdims=True)
    probs = (weights / total).astype(jnp.bfloat16)
    tiles = jnp.concatenate([labs[owners[b * CAND + j]] for j in range(CAND)], axis=0)
    result = jnp.dot(probs, tiles, preferred_element_type=jnp.float32)
    out[...] = result.astype(jnp.bfloat16)


def score(owners, fresh, counts, place, got, parts):
    return pl.pallas_call(
        score_kernel,
        out_shape=jax.ShapeDtypeStruct((ROWS, LAB), jnp.bfloat16),
        grid_spec=pltpu.PrefetchScalarGridSpec(
            num_scalar_prefetch=4,
            grid=(BLK_DEV,),
            in_specs=[HBM] * 20,
            out_specs=pl.BlockSpec((BR, LAB), lambda b, *_: (b, 0)),
            scratch_shapes=[
                pltpu.VMEM((NDP, TR, D), jnp.bfloat16),
                pltpu.VMEM((NDP, TR, LAB), jnp.bfloat16),
                pltpu.VMEM((2, BR, D), jnp.bfloat16),
                pltpu.VMEM((BR, CAND * TR), jnp.float32),
                pltpu.SemaphoreType.DMA((4, NDP)),
                pltpu.SemaphoreType.DMA((2, NZ)),
            ],
        ),
        compiler_params=pltpu.CompilerParams(
            dimension_semantics=("arbitrary",), vmem_limit_bytes=56 * 1024 * 1024
        ),
        cost_estimate=pl.CostEstimate(
            flops=2 * ROWS * CAND * TR * WIDE,
            bytes_accessed=NDP * TR * WIDE * 2 + ROWS * WIDE * 2,
            transcendentals=ROWS * CAND * TR,
        ),
    )(owners, fresh, counts, place, *got, *parts)


def body(embeddings, centroids, labels, candidates, counts, home):
    me = lax.axis_index("dp")
    z = lax.axis_index("mp")
    place = jnp.stack([me // (NY * NC), (me // NC) % NY, me % NC, z]).astype(jnp.int32)

    tiles = centroids.reshape(TILE_DEV, TR, D)
    tile_labels = labels.reshape(TILE_DEV, TR, LAB)
    own = [
        jnp.concatenate([tiles[:, s : s + HR], tile_labels[:, s : s + HR]], axis=2) for s in (0, HR)
    ]
    identity = jnp.arange(home.shape[0], dtype=jnp.int32)
    storage = jnp.sum(jnp.where(candidates[:, :, None] == identity, home, 0), axis=2)
    owner = storage // (TILE_DEV * NZ)
    local = storage % TILE_DEV
    hit = owner.reshape(-1)[:, None] == jnp.arange(NDP, dtype=jnp.int32)[None, :]
    wanted = jnp.max(jnp.where(hit, local.reshape(-1)[:, None], 0), axis=0)
    asked = jnp.broadcast_to(wanted[None, :], (NDP, NDP))
    table = lax.all_to_all(asked, "dp", split_axis=0, concat_axis=0, tiled=True)

    held = []
    for side in range(2):
        dx, dy = ((1, 0), (0, 1))[side]
        before = shift(own[side], dx, dy, 0)
        after = shift(own[side], -dx, -dy, 0)
        low, high, table = lax.optimization_barrier((before[:2], after[2:], table))
        low = shift(low, dx, dy, 0)
        high = shift(high, -dx, -dy, 0)
        held += [own[side], before, after, low, high]

    parts = [embeddings]
    for r in range(1, NZ):
        target = (z - r) % NZ
        piece = lax.dynamic_slice_in_dim(embeddings, target * ROWS, ROWS, 0)
        parts.append(lax.ppermute(piece, "mp", [(i, (i - r) % NZ) for i in range(NZ)]))

    got = [[None] * 8, [None] * 8]
    for targets in (((1, 0), (3, 0)), ((1, 1), (3, 1)), ((2, 0), (2, 1)), ((0, 0), (0, 1))):
        sends = pick(targets, table, place, held)
        for side in range(2):
            for i, (step, flip) in enumerate(targets):
                value = sends[side * len(targets) + i]
                if (step, flip) != (0, 0):
                    value = shift(value, step * side, step * (1 - side), flip)
                got[side][((-step) % 4) * 2 + flip] = value

    live = jnp.arange(CAND, dtype=jnp.int32)[None, :] < counts[:, None]
    slots = jnp.where(live, owner, owner[:, :1])
    flat = slots.reshape(-1)
    order = jnp.arange(BLK_DEV * CAND, dtype=jnp.int32) // CAND
    seen = (flat[:, None] == flat[None, :]) & (order[None, :] < order[:, None])
    fresh = (live.reshape(-1) & ~jnp.any(seen, axis=1)).astype(jnp.int32)
    return score(flat, fresh, counts, place, got[0] + got[1], parts)


def solution(mesh):
    placed = (
        P("dp", "mp"),
        P(("dp", "mp"), None),
        P(("dp", "mp"), None),
        P(("dp", "mp"), None),
        P(("dp", "mp")),
        P(),
    )
    return jax.shard_map(
        body, mesh=mesh, in_specs=placed, out_specs=P(("dp", "mp"), None), check_vma=False
    )
```

```python
import functools
import math

import jax
import jax.numpy as jnp
from jax import lax
from jax.experimental import pallas as pl
from jax.experimental.pallas import tpu as pltpu
from jax.sharding import PartitionSpec as P

D = 2560
LAB = 1024
TR = 128
HR = TR // 2
BR = 256
CAND = 8
NX = 4
NY = 4
NC = 2
NZ = 4
NDP = NX * NY * NC
TILE_DEV = 4
BLK_DEV = 8
PIECE = D // NZ
ROWS = BLK_DEV * BR
WIDE = D + LAB
NOTE = 128
MIB = 1024 * 1024
HBM = pl.BlockSpec(memory_space=pl.ANY)
SMEM = pl.BlockSpec(memory_space=pltpu.SMEM)


def dp_index(x, y, c):
    return ((x % NX) * NY + (y % NY)) * NC + c


def shift(value, dx, dy, flip):
    pairs = [
        (dp_index(x, y, c), dp_index(x + dx, y + dy, c ^ flip))
        for x in range(NX)
        for y in range(NY)
        for c in range(NC)
    ]
    return lax.ppermute(value, "dp", pairs)


class Lanes:
    def __init__(self):
        self.last = {}

    def send(self, value, dx, dy, flip=0):
        axis, step = ("x", dx % 4) if dx else ("y", dy % 4)
        lanes = [(axis, 1), (axis, 3)] if step == 2 else [(axis, step)]
        ends = [self.last[lane] for lane in lanes if lane in self.last]
        if ends:
            value, *_ = lax.optimization_barrier((value, *ends))
        out = shift(value, dx, dy, flip)
        if step != 2:
            self.last[lanes[0]] = out
        return out


def pick_kernel(jobs, which, table, place, *refs):
    outs = refs[-3 - len(jobs) : -3]
    stage, sem, out_sem = refs[-3:]
    x, y, c = place[0], place[1], place[2]
    moves = []
    for job, (side, step, flip, left, width) in enumerate(jobs):
        own, before, after, far = (refs[side * 8 + 2 * i : side * 8 + 2 * i + 2] for i in range(4))
        for r in which:
            if side == 0:
                owner = (((x + r) & 3) * NY + y) * NC + c
            else:
                owner = (x * NY + ((y + r) & 3)) * NC + c
            row = side * 2 + flip if step == 2 else side * 8 + step * 2 + flip
            w = table[row, owner]
            source = (own, after, far, before)[r]
            at = len(moves)
            room = stage.at[at, :, pl.ds(0, width)]
            columns = pl.ds(left, width)

            @pl.when(w < 2)
            def _():
                piece = source[0].at[jnp.minimum(w, 1), :, columns]
                pltpu.make_async_copy(piece, room, sem.at[at]).start()

            @pl.when(w >= 2)
            def _():
                piece = source[1].at[jnp.maximum(w - 2, 0), :, columns]
                pltpu.make_async_copy(piece, room, sem.at[at]).start()

            moves.append((room, own[0].at[0, :, columns], outs[job].at[which.index(r)]))
    for i, (room, piece, out) in enumerate(moves):
        pltpu.make_async_copy(piece, room, sem.at[i]).wait()
        pltpu.make_async_copy(room, out, out_sem.at[i]).start()
    for i, (room, piece, out) in enumerate(moves):
        pltpu.make_async_copy(room, out, out_sem.at[i]).wait()


def pick(jobs, table, place, held, which=(0, 1, 2, 3)):
    number = len(jobs) * len(which)
    widest = max(job[4] for job in jobs)
    return pl.pallas_call(
        functools.partial(pick_kernel, jobs, which),
        out_shape=[jax.ShapeDtypeStruct((len(which), HR, job[4]), jnp.bfloat16) for job in jobs],
        in_specs=[SMEM, SMEM] + [HBM] * len(held),
        out_specs=[HBM] * len(jobs),
        scratch_shapes=[
            pltpu.VMEM((number, HR, widest), jnp.bfloat16),
            pltpu.SemaphoreType.DMA((number,)),
            pltpu.SemaphoreType.DMA((number,)),
        ],
        compiler_params=pltpu.CompilerParams(vmem_limit_bytes=60 * MIB),
        cost_estimate=pl.CostEstimate(
            flops=0,
            bytes_accessed=sum(4 * len(which) * HR * job[4] for job in jobs),
            transcendentals=0,
        ),
    )(table, place, *held)


def half_copies(got, place, o, start):
    x, y, c = place[0], place[1], place[2]
    rx = ((o >> 3) - x) & 3
    ry = ((o >> 1) - y) & 3
    rc = (o & 1) ^ c
    for side, near, r in ((0, ry, rx), (1, rx, ry)):
        which = near * 2 + rc
        for k in range(8):
            if k in (2, 6):

                @pl.when((which == k) & (r != 2))
                def _():
                    start(side, got[side][k], jnp.where(r == 3, 2, r))

                @pl.when((which == k) & (r == 2))
                def _():
                    start(side, got[side][8 + k // 4], 0)
            else:

                @pl.when(which == k)
                def _():
                    start(side, got[side][k], r)


def probs_kernel(owners, counts, place, *refs):
    got = (refs[0:10], refs[10:20])
    features = refs[20]
    out = refs[-5]
    cents, rows, tile_sem, row_sem = refs[-4:]
    step = pl.program_id(0)

    def row_copies(at):
        slot = lax.rem(at, 2)
        for r in range(NZ):
            start = pl.multiple_of(r * ROWS + at * BR, BR)
            yield pltpu.make_async_copy(
                features.at[pl.ds(start, BR), :],
                rows.at[slot, :, pl.ds(r * PIECE, PIECE)],
                row_sem.at[slot, r],
            )

    def tile_copy(at, j, side, ref, r):
        slot = lax.rem(at, 2)
        return pltpu.make_async_copy(
            ref.at[r, :, pl.ds(0, D)], cents.at[slot, j, pl.ds(side * HR, HR), :], tile_sem.at[slot, j, side]
        )

    def fetch(at):
        for copy in row_copies(at):
            copy.start()

        def one(j, carry):
            @pl.when(j < counts[at])
            def _():
                o = owners[at * CAND + j]
                half_copies(
                    got, place, o, lambda side, ref, r: tile_copy(at, j, side, ref, r).start()
                )

            return carry

        lax.fori_loop(0, CAND, one, 0)

    @pl.when(step == 0)
    def _():
        fetch(step)

    @pl.when(step + 1 < BLK_DEV)
    def _():
        fetch(step + 1)

    live = counts[step]
    for copy in row_copies(step):
        copy.wait()
    for j in range(CAND):

        @pl.when(j < live)
        def _():
            for side in range(2):
                tile_copy(step, j, side, got[side][0], 0).wait()

    slot = lax.rem(step, 2)
    scale = 2.0 / math.sqrt(D)

    def attend(slots):
        tiles = cents[slot, 0:slots].reshape(slots * TR, D)
        value = lax.dot_general(
            rows[slot], tiles, (((1,), (1,)), ((), ())), preferred_element_type=jnp.float32
        )
        column = lax.broadcasted_iota(jnp.int32, (BR, slots * TR), 1)
        value = jnp.where(column < live * TR, value * scale, -jnp.inf)
        peak = jnp.max(value, axis=1, keepdims=True)
        weights = jnp.exp(value - peak)
        total = jnp.sum(weights, axis=1, keepdims=True)
        out[:, 0 : slots * TR] = (weights / total).astype(jnp.bfloat16)
        if slots < CAND:
            out[:, slots * TR :] = jnp.zeros((BR, (CAND - slots) * TR), jnp.bfloat16)

    @pl.when(live <= 4)
    def _():
        attend(4)

    @pl.when((live > 4) & (live <= 6))
    def _():
        attend(6)

    @pl.when(live > 6)
    def _():
        attend(8)


def probabilities(owners, counts, place, got, features):
    return pl.pallas_call(
        probs_kernel,
        out_shape=jax.ShapeDtypeStruct((ROWS, CAND * TR), jnp.bfloat16),
        grid_spec=pltpu.PrefetchScalarGridSpec(
            num_scalar_prefetch=3,
            grid=(BLK_DEV,),
            in_specs=[HBM] * 21,
            out_specs=pl.BlockSpec((BR, CAND * TR), lambda s, *_: (s, 0)),
            scratch_shapes=[
                pltpu.VMEM((2, CAND, TR, D), jnp.bfloat16),
                pltpu.VMEM((2, BR, D), jnp.bfloat16),
                pltpu.SemaphoreType.DMA((2, CAND, 2)),
                pltpu.SemaphoreType.DMA((2, NZ)),
            ],
        ),
        compiler_params=pltpu.CompilerParams(
            dimension_semantics=("arbitrary",), vmem_limit_bytes=60 * MIB
        ),
        cost_estimate=pl.CostEstimate(
            flops=2 * ROWS * CAND * TR * D,
            bytes_accessed=(BLK_DEV * CAND * TR * D + ROWS * D) * 2,
            transcendentals=ROWS * CAND * TR,
        ),
    )(owners, counts, place, *got, features)


def mix_kernel(owners, counts, place, *refs):
    got = (refs[0:10], refs[10:20])
    probs, out, labs, sem = refs[20:]
    b = pl.program_id(0)

    def tile_copy(at, j, side, ref, r):
        slot = lax.rem(at, 2)
        left = ref.shape[2] - LAB
        rows = pl.ds(pl.multiple_of(j * TR + side * HR, HR), HR)
        return pltpu.make_async_copy(
            ref.at[r, :, pl.ds(left, LAB)], labs.at[slot, rows, :], sem.at[slot, j, side]
        )

    def used(at):
        return ((counts[at] + 1) // 2) * 2

    def fetch(at):
        def one(j, carry):
            o = owners[at * CAND + j]
            half_copies(
                got, place, o, lambda side, ref, r: tile_copy(at, j, side, ref, r).start()
            )
            return carry

        lax.fori_loop(0, used(at), one, 0)

    @pl.when(b == 0)
    def _():
        fetch(b)

    @pl.when(b + 1 < BLK_DEV)
    def _():
        fetch(b + 1)

    slots_used = used(b)
    for j in range(CAND):

        @pl.when(j < slots_used)
        def _():
            for side in range(2):
                tile_copy(b, j, side, got[side][0], 0).wait()

    slot = lax.rem(b, 2)

    def mix(slots):
        value = jnp.dot(
            probs[:, 0 : slots * TR], labs[slot, 0 : slots * TR], preferred_element_type=jnp.float32
        )
        out[...] = value.astype(jnp.bfloat16)

    for slots in (4, 6, 8):

        @pl.when(slots_used == slots)
        def _():
            mix(slots)


def mixture(owners, counts, place, got, probs):
    return pl.pallas_call(
        mix_kernel,
        out_shape=jax.ShapeDtypeStruct((ROWS, LAB), jnp.bfloat16),
        grid_spec=pltpu.PrefetchScalarGridSpec(
            num_scalar_prefetch=3,
            grid=(BLK_DEV,),
            in_specs=[HBM] * 20 + [pl.BlockSpec((BR, CAND * TR), lambda b, *_: (b, 0))],
            out_specs=pl.BlockSpec((BR, LAB), lambda b, *_: (b, 0)),
            scratch_shapes=[
                pltpu.VMEM((2, CAND * TR, LAB), jnp.bfloat16),
                pltpu.SemaphoreType.DMA((2, CAND, 2)),
            ],
        ),
        compiler_params=pltpu.CompilerParams(
            dimension_semantics=("arbitrary",), vmem_limit_bytes=60 * MIB
        ),
        cost_estimate=pl.CostEstimate(
            flops=2 * ROWS * CAND * TR * LAB,
            bytes_accessed=(BLK_DEV * CAND * TR * LAB + 2 * ROWS * LAB) * 2,
            transcendentals=0,
        ),
    )(owners, counts, place, *got, probs)


def jobs_of(step, left=0, width=WIDE, flips=(0, 1)):
    return tuple((side, s, flip, left, width) for flip in flips for side in range(2) for s in step)


NEAR = jobs_of((1, 3), flips=(0,))
CROSS = jobs_of((1, 3), flips=(1,))
HOME = jobs_of((0,))
FAR = jobs_of((2,), 0, D)
FAR_LABELS = jobs_of((2,), D, LAB)


def body(embeddings, centroids, labels, candidates, counts, home):
    me = lax.axis_index("dp")
    z = lax.axis_index("mp")
    place = jnp.stack([me // (NY * NC), (me // NC) % NY, me % NC, z]).astype(jnp.int32)
    line = Lanes()

    features = lax.all_to_all(embeddings, "mp", split_axis=0, concat_axis=0, tiled=True)

    identity = jnp.arange(home.shape[0], dtype=jnp.int32)
    storage = jnp.sum(jnp.where(candidates[:, :, None] == identity, home, 0), axis=2)
    owner = storage // (TILE_DEV * NZ)
    local = storage % TILE_DEV
    hit = owner.reshape(-1)[:, None] == jnp.arange(NDP, dtype=jnp.int32)[None, :]
    wanted = jnp.max(jnp.where(hit, local.reshape(-1)[:, None], 0), axis=0)
    note = jnp.pad(wanted, (0, NOTE - NDP)).astype(jnp.bfloat16)
    note = jnp.broadcast_to(note, (2, HR, NOTE))

    tiles = centroids.reshape(TILE_DEV, TR, D)
    tile_labels = labels.reshape(TILE_DEV, TR, LAB)
    ways = ((1, 0), (0, 1))
    own = [
        [
            jnp.concatenate(
                [a[t : t + 2, s * HR : (s + 1) * HR] for a in (tiles, tile_labels)] + [note], axis=2
            )
            for t in (0, 2)
        ]
        for s in range(2)
    ]
    before, after, far = ([[None, None] for _ in range(2)] for _ in range(3))
    for s, (dx, dy) in enumerate(ways):
        before[s][0] = line.send(own[s][0], dx, dy)
        after[s][1] = line.send(own[s][1], -dx, -dy)
    for s, (dx, dy) in enumerate(ways):
        before[s][1] = line.send(own[s][1], dx, dy)
        after[s][0] = line.send(own[s][0], -dx, -dy)

    def read(piece):
        return piece[0, 0, WIDE : WIDE + NDP].astype(jnp.int32)

    def swap(wishes):
        return lax.ppermute(wishes, "dp", [(i, i ^ 1) for i in range(NDP)])

    blank = jnp.zeros((NDP,), jnp.int32)
    near = [[wanted, read(after[1 - s][1]), blank, read(before[1 - s][0])] for s in range(2)]
    table = jnp.stack([row for s in range(2) for v in near[s] for row in (v, blank)])
    crossed = swap(jnp.stack(near[0] + near[1]))

    for s, (dx, dy) in enumerate(ways):
        far[s][0] = line.send(before[s][0], dx, dy)
        far[s][1] = line.send(after[s][1], -dx, -dy)

    def exchange(jobs, sends, got):
        for (side, step, flip, _, _), value in zip(jobs, sends, strict=True):
            if (step, flip) != (0, 0):
                value = line.send(value, step * side, step * (1 - side), flip)
            got[side][((-step) % 4) * 2 + flip] = value

    got = [[None] * 10, [None] * 10]
    held = [h for s in range(2) for h in own[s] + before[s] + after[s] + own[s]]
    exchange(NEAR, pick(NEAR, table, place, held, (0, 1, 3)), got)
    held = [h for s in range(2) for h in own[s] + before[s] + after[s] + far[s]]
    rest = pick(NEAR, table, place, held, (2,))
    crossed, *rest = lax.optimization_barrier((crossed, *rest))
    crossed = jnp.repeat(crossed, 2, axis=0)
    odd = (jnp.arange(16, dtype=jnp.int32) % 2 == 1)[:, None]
    sends = pick(CROSS + HOME, jnp.where(odd, crossed, table), place, held)
    distant = jnp.stack([read(far[1][0]), read(far[0][0])])
    distant = jnp.stack([distant, swap(distant)], axis=1).reshape(4, NDP)
    later = pick(FAR + FAR_LABELS, distant, place, held)
    rest[-1], sends, later = lax.optimization_barrier((rest[-1], sends, later))
    for (side, step, flip, _, _), value in zip(NEAR, rest, strict=True):
        got[side][9 - step // 2] = line.send(value, step * side, step * (1 - side), flip)
    exchange(CROSS + HOME, sends, got)
    exchange(FAR, later[: len(FAR)], got)
    got_labels = [list(g) for g in got]
    later, *_ = lax.optimization_barrier((later[len(FAR) :], got[0][4], got[0][5], got[1][4], got[1][5]))
    exchange(FAR_LABELS, later, got_labels)

    live = jnp.arange(CAND, dtype=jnp.int32)[None, :] < counts[:, None]
    slots = jnp.where(live, owner, owner[:, :1])
    flat = slots.reshape(-1)
    probs = probabilities(flat, counts, place, got[0] + got[1], features)
    return mixture(flat, counts, place, got_labels[0] + got_labels[1], probs)


def solution(mesh):
    placed = (
        P("dp", "mp"),
        P(("dp", "mp"), None),
        P(("dp", "mp"), None),
        P(("dp", "mp"), None),
        P(("dp", "mp")),
        P(),
    )
    return jax.shard_map(
        body, mesh=mesh, in_specs=placed, out_specs=P(("dp", "mp"), None), check_vma=False
    )
```
